128 devices in a mesh: lon: 32 (over z, y, x_hi), lat: 4 (over x_lo, core).
Axes of the slice: x: 4 (x_hi: 2, x_lo: 2; x = x_hi * 2 + x_lo), y: 4, z: 4, core: 2. Of those that a mesh axis runs over, the one named last changes fastest.
Arguments:
- noise: bfloat16 [2, 4, 4096, 8192], P(None, None, 'lat', 'lon'), may hold values from -6 to 6
- factors: bfloat16 [9, 32, 256, 256], P(None, 'lat'), may hold values from -0.125 to 0.125
- tile_mask: int32 [9, 32, 2, 2], P(None, 'lat'), may hold values 0 or 1
- lat_weights: float32 [5, 4096], P(None, 'lat'), may hold values from 0.2 to 1
Outputs:
- result_field: float32 [2, 4, 4096, 8192], P(None, None, 'lat', 'lon')
The draws below stay inside these ranges and needn't reach their ends.
All inputs are finite; a program needn't handle non-finite values. No bound on the sum of `tile_mask` on one device may be relied on, other than what follows from the above.
Results may differ from the reference program's by a relative error of at most 0.0003.
Values may be sent and summed in bfloat16 or wider, within the bound.
No kernel may reach another device: no remote copies, remote signals or barrier semaphores. Data moves between devices by JAX's collectives and lax.ppermute only.
A program may use at most 192 MiB of HBM per device.

```python
import jax
import jax.numpy as jnp

LON_DEV = 256
TILE = 128
BAND = 128
LEV = 4
MEMBERS = 2
MAXLAG = 4
RIM = 2
NLAG = 9
LON = 8192
LAT = 4096
BANDS = 32
TILES = 2
N_LON = 32


def place_ends(drawn, rng, least, top_value):
    extent = drawn.shape
    place = [jax.random.randint(jax.random.fold_in(rng, axis), (), 0, extent[axis]) for axis in range(len(extent))]
    drawn = drawn.at[tuple(place)].set(least)
    longest = extent.index(max(extent))
    place[longest] = (place[longest] + 1) % extent[longest]
    return drawn.at[tuple(place)].set(top_value)


def level_of(rng, dims, pieces, least, top_value):
    def one(dim, blocks):
        draws = jax.random.uniform(jax.random.fold_in(jax.random.fold_in(rng, 6), dim), (blocks,), jnp.float32, least / len(pieces), top_value / len(pieces))
        return jnp.repeat(jnp.exp(draws), dims[dim] // blocks).reshape((-1,) + (1,) * (len(dims) - dim - 1))

    loudness = one(*pieces[0])
    for cut in pieces[1:]:
        loudness = loudness * one(*cut)
    return loudness


def gaussian(own_key, extent, deviation, reach, shards=(), held_as=jnp.bfloat16):
    result = jax.random.normal(own_key, extent, jnp.float32) * deviation
    if len(shards) > 0:
        result = level_of(own_key, extent, shards, -0.22, 0.18) * result
    return jnp.clip(result, min=-reach, max=reach).astype(held_as)


def setup_inputs(seed: int = 0) -> dict:
    streams_of = jax.random.split(jax.random.key(seed), 5)
    return {
        "noise": gaussian(streams_of[0], (MEMBERS, LEV, LAT, LON), 1.0, 6.0, ((2, 4), (3, 32))),
        "factors": gaussian(streams_of[1], (NLAG, BANDS, LON_DEV, LON_DEV), (NLAG * LON_DEV) ** -0.5, 0.125, ((1, 4),)),
        "tile_mask": place_ends((jax.random.randint(streams_of[2], (NLAG, BANDS, TILES, TILES), 0, 3) < 2).astype(jnp.int32), jax.random.fold_in(streams_of[2], 1), 0, 1),
        "lat_weights": jnp.clip(0.2 + 0.8 * jax.random.uniform(streams_of[3], (2 * RIM + 1, LAT), jnp.float32) ** level_of(streams_of[3], (2 * RIM + 1, LAT), ((1, 4),), -0.2, 0.2), 0.2, 1.0),
    }


def reference(noise, factors, tile_mask, lat_weights):
    tile_ones = tile_mask.astype(jnp.bfloat16)
    blocks = (factors.reshape(NLAG, BANDS, TILES, TILE, TILES, TILE) * tile_ones[:, :, :, None, :, None]).reshape(NLAG, BANDS, LON_DEV, LON_DEV)
    mixture = jnp.zeros((MEMBERS, LEV, LAT, LON), jnp.float32)
    for offset in range(-MAXLAG, MAXLAG + 1):
        rolled = jnp.roll(noise, -offset * LON_DEV, axis=3).reshape(MEMBERS, LEV, BANDS, BAND, N_LON, LON_DEV)
        product = jnp.einsum("mvbyqj,bji->mvbyqi", rolled.astype(jnp.float32), blocks[offset + MAXLAG].astype(jnp.float32))
        mixture = mixture + product.reshape(MEMBERS, LEV, LAT, LON)
    padded = jnp.pad(mixture, ((0, 0), (0, 0), (RIM, RIM), (0, 0)))
    result_field = lat_weights[0][None, None, :, None] * padded[:, :, 0:LAT]
    for row_shift in range(1, 2 * RIM + 1):
        result_field = result_field + lat_weights[row_shift][None, None, :, None] * padded[:, :, row_shift:row_shift + LAT]
    return result_field
```

```python
import functools

import jax
import jax.numpy as jnp
from jax import lax
from jax.experimental import pallas as pl
from jax.experimental.pallas import tpu as pltpu
from jax.sharding import PartitionSpec as P

TILE = 128
RIM = 2
TOP = 32767.0
PACK = 16


def mix_kernel(bands, quarter, mask_ref, noise_ref, factors_ref, out_ref, weights):
    lags, _, width, _ = factors_ref.shape
    count, rows, _ = noise_ref.shape
    reach = lags // 2
    band = pl.program_id(0)
    tiles = width // TILE
    local_band = quarter[0] * pl.num_programs(0) + band
    for lag in range(lags):
        for a in range(tiles):
            for b in range(tiles):
                place = ((lag * bands + local_band) * tiles + a) * tiles + b
                keep = mask_ref[place].astype(jnp.float32).astype(jnp.bfloat16)
                weights[pl.ds(lag * width + a * TILE, TILE), pl.ds(b * TILE, TILE)] = (
                    factors_ref[lag, 0, pl.ds(a * TILE, TILE), pl.ds(b * TILE, TILE)] * keep
                )

    @pl.loop(0, count)
    def _(c):
        total = jnp.zeros((rows, width), jnp.float32)
        for lag in range(lags):
            source = lax.rem(c + (lag - reach) + count, count)
            total += jnp.dot(
                noise_ref[source],
                weights[pl.ds(lag * width, width), :],
                preferred_element_type=jnp.float32,
            )
        peak = jnp.maximum(jnp.max(jnp.abs(total), axis=0, keepdims=True), 2.0**-120)
        power = jnp.ceil(jnp.log2(peak) + 1e-5)
        coded = jnp.round(total * jnp.exp2(-power) * TOP)
        out_ref[c, pl.ds(0, rows), :] = coded.astype(jnp.int32).astype(jnp.int16)
        out_ref[c, pl.ds(rows, PACK), :] = (
            jnp.broadcast_to(power, (PACK, width)).astype(jnp.int32).astype(jnp.int16)
        )


def mix(quarter, mask, noise, factors):
    count, rows, width = noise.shape
    lags, bands = factors.shape[:2]
    parts = rows // TILE
    return pl.pallas_call(
        functools.partial(mix_kernel, bands),
        out_shape=jax.ShapeDtypeStruct((count, parts, TILE + PACK, width), jnp.int16),
        grid_spec=pltpu.PrefetchScalarGridSpec(
            num_scalar_prefetch=2,
            grid=(parts,),
            in_specs=[
                pl.BlockSpec((count, TILE, width), lambda b, quarter, mask: (0, b, 0)),
                pl.BlockSpec(
                    (lags, 1, width, width),
                    lambda b, quarter, mask: (0, quarter[0] * parts + b, 0, 0),
                ),
            ],
            out_specs=pl.BlockSpec(
                (count, None, TILE + PACK, width), lambda b, quarter, mask: (0, b, 0, 0)
            ),
            scratch_shapes=[pltpu.VMEM((lags * width, width), jnp.bfloat16)],
        ),
        compiler_params=pltpu.CompilerParams(vmem_limit_bytes=48 * 2**20),
    )(quarter, mask, noise, factors)


def filter_kernel(coded_ref, low_ref, high_ref, lat_weights_ref, out_ref, padded, spread):
    blocks, _, width = coded_ref.shape
    rows = out_ref.shape[0]
    taps = spread.shape[0]

    @pl.when(pl.program_id(0) == 0)
    def _():
        for tap in range(taps):
            spread[tap] = jnp.broadcast_to(lat_weights_ref[:, tap : tap + 1], spread.shape[1:])

    padded[pl.ds(0, 8), :] = low_ref[...]
    padded[pl.ds(8 + rows, 8), :] = high_ref[...]
    for block in range(blocks):
        power = coded_ref[block, pl.ds(TILE, PACK), :].astype(jnp.float32)[0:1]
        scale = jnp.exp2(power) * (1.0 / TOP)
        padded[pl.ds(8 + block * TILE, TILE), :] = (
            coded_ref[block, pl.ds(0, TILE), :].astype(jnp.float32) * scale
        )
    for block in range(blocks):
        for half in range(width // TILE):
            lanes = pl.ds(half * TILE, TILE)
            total = jnp.zeros((TILE, TILE), jnp.float32)
            for tap in range(taps):
                total += (
                    spread[tap, pl.ds(block * TILE, TILE), :]
                    * padded[pl.ds(8 - RIM + tap + block * TILE, TILE), lanes]
                )
            out_ref[pl.ds(block * TILE, TILE), lanes] = total


def band_filter(coded, low, high, lat_weights):
    fields, blocks, _, width = coded.shape
    rows = blocks * TILE
    taps = lat_weights.shape[0]
    return pl.pallas_call(
        filter_kernel,
        out_shape=jax.ShapeDtypeStruct((fields, rows, width), jnp.float32),
        grid=(fields,),
        in_specs=[
            pl.BlockSpec((None, blocks, TILE + PACK, width), lambda f: (f, 0, 0, 0)),
            pl.BlockSpec((None, 8, width), lambda f: (f, 0, 0)),
            pl.BlockSpec((None, 8, width), lambda f: (f, 0, 0)),
            pl.BlockSpec((rows, taps), lambda f: (0, 0)),
        ],
        out_specs=pl.BlockSpec((None, rows, width), lambda f: (f, 0, 0)),
        scratch_shapes=[
            pltpu.VMEM((rows + 16, width), jnp.float32),
            pltpu.VMEM((taps, rows, TILE), jnp.float32),
        ],
        compiler_params=pltpu.CompilerParams(vmem_limit_bytes=48 * 2**20),
    )(coded, low, high, lat_weights.T)


def edge(coded, block, start):
    scale = jnp.exp2(coded[:, block, TILE : TILE + 1].astype(jnp.float32)) * (1.0 / TOP)
    return coded[:, block, start : start + RIM].astype(jnp.float32) * scale


def per_device(noise, factors, tile_mask, lat_weights):
    members, levels, rows, width = noise.shape
    fields = members * levels
    count = lax.axis_size("lon")
    quarters = count // fields
    quarter = (lax.axis_index("lon") % quarters).astype(jnp.int32).reshape(1)
    mine = lax.all_to_all(
        noise.reshape(count, rows // quarters, width), "lon", 0, 0, tiled=True
    )
    sent = mix(quarter, tile_mask.reshape(-1), mine, factors)
    coded = lax.all_to_all(sent, "lon", 0, 0, tiled=True)
    coded = coded.reshape(fields, rows // TILE, TILE + PACK, width)
    lat = lax.axis_size("lat")
    forward = [(i, i + 1) for i in range(lat - 1)]
    backward = [(i + 1, i) for i in range(lat - 1)]
    low = lax.ppermute(edge(coded, -1, TILE - RIM), "lat", forward)
    high = lax.ppermute(edge(coded, 0, 0), "lat", backward)
    low = jnp.pad(low, ((0, 0), (8 - RIM, 0), (0, 0)))
    high = jnp.pad(high, ((0, 0), (0, 8 - RIM), (0, 0)))
    result_field = band_filter(coded, low, high, lat_weights)
    return result_field.reshape(members, levels, rows, width)


def solution(mesh):
    return jax.shard_map(
        per_device,
        mesh=mesh,
        in_specs=(
            P(None, None, "lat", "lon"),
            P(None, "lat", None, None),
            P(None, "lat", None, None),
            P(None, "lat"),
        ),
        out_specs=P(None, None, "lat", "lon"),
        check_vma=False,
    )
```

```python
import functools

import jax
import jax.numpy as jnp
from jax import lax
from jax.experimental import pallas as pl
from jax.experimental.pallas import tpu as pltpu
from jax.sharding import PartitionSpec as P

TILE = 128
RIM = 2
TOP = 32767.0
SIDE = 16
GROUP = 8


def weights_kernel(place_ref, mask_ref, factors_ref, weights_ref):
    lags, _, width, _ = factors_ref.shape
    tiles = width // TILE
    band = place_ref[0] + pl.program_id(0)
    for lag in range(lags):
        for a in range(tiles):
            for b in range(tiles):
                index = ((lag * place_ref[1] + band) * tiles + a) * tiles + b
                keep = mask_ref[index].astype(jnp.float32).astype(jnp.bfloat16)
                weights_ref[lag, pl.ds(a * TILE, TILE), pl.ds(b * TILE, TILE)] = (
                    factors_ref[lag, 0, pl.ds(a * TILE, TILE), pl.ds(b * TILE, TILE)] * keep
                )


def masked_weights(place, mask, factors, parts):
    lags, _, width, _ = factors.shape
    return pl.pallas_call(
        weights_kernel,
        out_shape=jax.ShapeDtypeStruct((parts, lags, width, width), factors.dtype),
        grid_spec=pltpu.PrefetchScalarGridSpec(
            num_scalar_prefetch=2,
            grid=(parts,),
            in_specs=[
                pl.BlockSpec(
                    (lags, 1, width, width), lambda b, place, mask: (0, place[0] + b, 0, 0)
                )
            ],
            out_specs=pl.BlockSpec(
                (None, lags, width, width), lambda b, place, mask: (b, 0, 0, 0)
            ),
        ),
        compiler_params=pltpu.CompilerParams(vmem_limit_bytes=12 * 2**20),
    )(place, mask, factors)


def mix_kernel(group, place_ref, noise_ref, weights_ref, coded_ref):
    lags, width, _ = weights_ref.shape
    count, rows, _ = noise_ref.shape
    reach = lags // 2
    halves = width // TILE
    step = pl.program_id(1)
    total = None
    for lag in range(lags):
        source = jnp.concatenate(
            [
                noise_ref[lax.rem(step * group + g + (lag - reach) + count, count)]
                for g in range(group)
            ],
            axis=0,
        )
        product = jnp.dot(source, weights_ref[lag], preferred_element_type=jnp.float32)
        total = product if total is None else total + product
    for g in range(group):
        powers, edges = [], []
        for half in range(halves):
            block = total[g * rows : (g + 1) * rows, half * TILE : (half + 1) * TILE]
            peak = jnp.maximum(jnp.max(jnp.abs(block), axis=0, keepdims=True), 2.0**-120)
            power = jnp.ceil(jnp.log2(peak) + 1e-5)
            coded = jnp.round(block * jnp.exp2(-power) * TOP).astype(jnp.int32)
            coded_ref[g, half * rows : (half + 1) * rows, :] = coded.astype(jnp.int16)
            powers.append(power.astype(jnp.int32))
            edges.append(jnp.where(place_ref[3] == 1, coded[rows - RIM :], coded[:RIM]))
        empty = jnp.zeros((SIDE // 2 - halves, TILE), jnp.int32)
        side = powers + [empty] + powers + edges + [empty[: SIDE // 2 - halves * (1 + RIM)]]
        coded_ref[g, halves * rows :, :] = jnp.concatenate(side, axis=0).astype(jnp.int16)


def mix(place, noise, weights):
    count, rows, width = noise.shape
    parts, lags = weights.shape[:2]
    rows = rows // parts
    sent = rows * width // TILE + SIDE
    return pl.pallas_call(
        functools.partial(mix_kernel, GROUP),
        out_shape=jax.ShapeDtypeStruct((count, parts, sent, TILE), jnp.int16),
        grid_spec=pltpu.PrefetchScalarGridSpec(
            num_scalar_prefetch=1,
            grid=(parts, count // GROUP),
            in_specs=[
                pl.BlockSpec((count, rows, width), lambda b, s, place: (0, b, 0)),
                pl.BlockSpec((None, lags, width, width), lambda b, s, place: (b, 0, 0, 0)),
            ],
            out_specs=pl.BlockSpec((GROUP, None, sent, TILE), lambda b, s, place: (s, b, 0, 0)),
        ),
        compiler_params=pltpu.CompilerParams(vmem_limit_bytes=28 * 2**20),
        cost_estimate=pl.CostEstimate(
            flops=2 * lags * count * rows * parts * width * width,
            bytes_accessed=4 * count * rows * parts * width,
            transcendentals=0,
        ),
    )(place, noise, weights)


def filter_kernel(coded_ref, lat_ref, out_ref, padded, spread):
    bands, _, _ = coded_ref.shape
    rows, width = out_ref.shape
    halves = width // TILE
    strip = rows // bands
    taps = spread.shape[0]

    @pl.when(pl.program_id(0) == 0)
    def _():
        for tap in range(taps):
            spread[tap] = jnp.broadcast_to(lat_ref[:, tap : tap + 1], spread.shape[1:])

    for band in range(bands):
        side = coded_ref[band, halves * strip :].astype(jnp.float32)
        for half in range(halves):
            lanes = pl.ds(half * TILE, TILE)
            scale = jnp.exp2(side[half : half + 1]) * (1.0 / TOP)
            padded[pl.ds(8 + band * strip, strip), lanes] = (
                coded_ref[band, half * strip : (half + 1) * strip].astype(jnp.float32) * scale
            )
            if band in (0, bands - 1):
                start = SIDE // 2
                scale = jnp.exp2(side[start + half : start + half + 1]) * (1.0 / TOP)
                start += halves + half * RIM
                place = 8 - RIM if band == 0 else 8 + rows
                padded[place : place + RIM, lanes] = side[start : start + RIM] * scale
    for band in range(bands):
        for half in range(halves):
            lanes = pl.ds(half * TILE, TILE)
            total = jnp.zeros((strip, TILE), jnp.float32)
            for tap in range(taps):
                total += (
                    spread[tap, pl.ds(band * strip, strip), :]
                    * padded[pl.ds(8 - RIM + tap + band * strip, strip), lanes]
                )
            out_ref[pl.ds(band * strip, strip), lanes] = total


def band_filter(coded, lat_weights, width):
    fields, bands, sent, _ = coded.shape
    rows, taps = lat_weights.shape
    return pl.pallas_call(
        filter_kernel,
        out_shape=jax.ShapeDtypeStruct((fields, rows, width), jnp.float32),
        grid=(fields,),
        in_specs=[
            pl.BlockSpec((None, bands, sent, TILE), lambda f: (f, 0, 0, 0)),
            pl.BlockSpec((rows, taps), lambda f: (0, 0)),
        ],
        out_specs=pl.BlockSpec((None, rows, width), lambda f: (f, 0, 0)),
        scratch_shapes=[
            pltpu.VMEM((rows + 16, width), jnp.float32),
            pltpu.VMEM((taps, rows, TILE), jnp.float32),
        ],
        compiler_params=pltpu.CompilerParams(vmem_limit_bytes=20 * 2**20),
        cost_estimate=pl.CostEstimate(
            flops=10 * fields * rows * width,
            bytes_accessed=6 * fields * rows * width,
            transcendentals=0,
        ),
    )(coded, lat_weights)


def per_device(noise, factors, tile_mask, lat_weights):
    members, levels, rows, width = noise.shape
    fields = members * levels
    bands = factors.shape[1]
    count, lat = lax.axis_size("lon"), lax.axis_size("lat")
    strip = rows // bands
    parts = fields * bands // count
    shares = bands // parts
    share = (lax.axis_index("lon") % shares).astype(jnp.int32)
    top = (share == shares - 1).astype(jnp.int32)
    place = jnp.stack([share * parts, jnp.int32(bands), top * (parts - 1), top])
    joins = []
    for field in range(fields):
        for row in range(lat - 1):
            south = (field * shares + shares - 1) * lat + row
            north = field * shares * lat + row + 1
            joins += [(south, north), (north, south)]
    weights = masked_weights(place, tile_mask.reshape(-1), factors, parts)
    mine = lax.all_to_all(
        noise.reshape(count, parts * strip, width), "lon", 0, 0, tiled=True
    )
    lat_weights = lat_weights.T
    mine, weights, lat_weights = lax.optimization_barrier((mine, weights, lat_weights))
    coded = mix(place, mine, weights)
    spot = (0, place[2], coded.shape[2] - SIDE, 0)
    side = lax.dynamic_slice(coded, spot, (count, 1, SIDE, TILE))
    other = lax.ppermute(side, ("lon", "lat"), joins)
    side = jnp.where(jnp.arange(SIDE)[None, None, :, None] < SIDE // 2, side, other)
    coded = lax.dynamic_update_slice(coded, side, spot)
    coded = lax.all_to_all(coded, "lon", 0, 0, tiled=True)
    coded = coded.reshape(fields, bands, -1, TILE)
    result_field = band_filter(coded, lat_weights, width)
    return result_field.reshape(members, levels, rows, width)


def solution(mesh):
    return jax.shard_map(
        per_device,
        mesh=mesh,
        in_specs=(
            P(None, None, "lat", "lon"),
            P(None, "lat", None, None),
            P(None, "lat", None, None),
            P(None, "lat"),
        ),
        out_specs=P(None, None, "lat", "lon"),
        check_vma=False,
    )
```

```python
import functools

import jax
import jax.numpy as jnp
from jax import lax
from jax.experimental import pallas as pl
from jax.experimental.pallas import tpu as pltpu
from jax.sharding import PartitionSpec as P

TILE = 128
RIM = 2
TOP = 32767.0
SIDE = 16
GROUP = 8


def device_at(place):
    return ((place // 8 + place // 2) % 4) * 8 + place % 8


def place_of(device):
    return ((device // 8 + 4 - device // 2 % 4) % 4) * 8 + device % 8


def code(block):
    peak = jnp.maximum(jnp.max(jnp.abs(block), axis=0, keepdims=True), 2.0**-120)
    power = jnp.ceil(jnp.log2(peak) + 1e-5)
    return jnp.round(block * jnp.exp2(-power) * TOP).astype(jnp.int32), power.astype(jnp.int32)


def fill_places(places, count, reach):
    for index in range(count + 2 * reach):
        places[index] = place_of((index + count - reach) % count)


def banded(places, noise_ref, weights, start, group, lines):
    lags = len(weights)
    targets = [device_at(start + g) for g in range(group)]
    total = None
    for lag in range(lags):
        blocks = [noise_ref[places[target + lag], lines, :] for target in targets]
        product = jnp.dot(
            jnp.concatenate(blocks, axis=0), weights[lag][...], preferred_element_type=jnp.float32
        )
        total = product if total is None else total + product
    return total


def rim_kernel(
    shares, mask_ref, noise_ref, factors_ref, side_ref, weights_ref, loaded, sems, places
):
    parts, lags, width, _ = weights_ref.shape
    count, rows, _ = noise_ref.shape
    tiles = width // TILE
    share = place_of(lax.axis_index("lon")) % shares
    last = share == shares - 1
    copies = [
        pltpu.make_async_copy(
            factors_ref.at[:, share * parts + part], loaded.at[part], sems.at[part]
        )
        for part in range(parts)
    ]
    for copy in copies:
        copy.start()
    fill_places(places, count, lags // 2)
    for part in range(parts):
        copies[part].wait()
        for lag in range(lags):
            for a in range(tiles):
                for b in range(tiles):
                    keep = mask_ref[share * parts + part, a, b, lag]
                    keep = keep.astype(jnp.float32).astype(jnp.bfloat16)
                    spot = (pl.ds(a * TILE, TILE), pl.ds(b * TILE, TILE))
                    weights_ref[(part, lag, *spot)] = loaded[(part, lag, *spot)] * keep
    weights = [weights_ref.at[jnp.where(last, parts - 1, 0), lag] for lag in range(lags)]
    line = pl.multiple_of(jnp.where(last, rows - SIDE, 0), SIDE)
    total = banded(places, noise_ref, weights, 0, count, pl.ds(line, SIDE))
    for g in range(count):
        block = total[g * SIDE : (g + 1) * SIDE]
        edge = jnp.where(last, block[SIDE - RIM :], block[:RIM])
        powers, codes = [], []
        for half in range(width // TILE):
            coded, power = code(edge[:, half * TILE : (half + 1) * TILE])
            powers.append(power)
            codes.append(coded)
        empty = jnp.zeros((SIDE - 3 * len(codes), TILE), jnp.int32)
        side_ref[g] = jnp.concatenate([empty] + powers + codes, axis=0).astype(jnp.int16)


def rim(mask, noise, factors, parts, shares):
    count, _, width = noise.shape
    lags = factors.shape[0]
    vmem = pl.BlockSpec(memory_space=pltpu.VMEM)
    held = (parts, lags, width, width)
    return pl.pallas_call(
        functools.partial(rim_kernel, shares),
        out_shape=[
            jax.ShapeDtypeStruct((count, SIDE, TILE), jnp.int16),
            jax.ShapeDtypeStruct(held, factors.dtype),
        ],
        in_specs=[
            pl.BlockSpec(memory_space=pltpu.SMEM),
            vmem,
            pl.BlockSpec(memory_space=pltpu.HBM),
        ],
        out_specs=[vmem] * 2,
        scratch_shapes=[
            pltpu.VMEM(held, factors.dtype),
            pltpu.SemaphoreType.DMA((parts,)),
            pltpu.SMEM((count + lags - 1,), jnp.int32),
        ],
        compiler_params=pltpu.CompilerParams(vmem_limit_bytes=46 * 2**20),
        cost_estimate=pl.CostEstimate(
            flops=2 * lags * count * SIDE * width * width,
            bytes_accessed=4 * count * SIDE * width,
            transcendentals=0,
        ),
    )(mask, noise, factors)


def mix_kernel(noise_ref, weights_ref, coded_ref, powers, places):
    parts, lags, width, _ = weights_ref.shape
    count, rows, _ = noise_ref.shape
    strip = rows // parts
    group = powers.shape[0] // parts
    halves = width // TILE
    part, step = pl.program_id(1), pl.program_id(0)

    @pl.when((part == 0) & (step == 0))
    def _():
        fill_places(places, count, lags // 2)

    weights = [weights_ref.at[part, lag] for lag in range(lags)]
    lines = pl.ds(pl.multiple_of(part * strip, strip), strip)
    total = banded(places, noise_ref, weights, step * group, group, lines)
    for g in range(group):
        block = total[g * strip : (g + 1) * strip]
        for half in range(halves):
            coded, power = code(block[:, half * TILE : (half + 1) * TILE])
            start = pl.multiple_of((part * halves + half) * strip, strip)
            coded_ref[step * group + g, pl.ds(start, strip), :] = coded.astype(jnp.int16)
            powers[part * group + g, half : half + 1, :] = power

    @pl.when(part == parts - 1)
    def _():
        for g in range(group):
            side = [powers[p * group + g, :halves] for p in range(parts)]
            side.append(jnp.zeros((SIDE - parts * halves, TILE), jnp.int32))
            coded_ref[step * group + g, parts * halves * strip :, :] = jnp.concatenate(side, axis=0).astype(
                jnp.int16
            )


def mix(noise, weights):
    count, rows, width = noise.shape
    parts, lags = weights.shape[:2]
    strip = rows // parts
    sent = rows * width // TILE + SIDE
    return pl.pallas_call(
        mix_kernel,
        out_shape=jax.ShapeDtypeStruct((count, sent, TILE), jnp.int16),
        grid=(count // GROUP, parts),
        in_specs=[pl.BlockSpec(memory_space=pltpu.VMEM)] * 2,
        out_specs=pl.BlockSpec(memory_space=pltpu.VMEM),
        scratch_shapes=[
            pltpu.VMEM((parts * GROUP, 8, TILE), jnp.int32),
            pltpu.SMEM((count + lags - 1,), jnp.int32),
        ],
        compiler_params=pltpu.CompilerParams(vmem_limit_bytes=16 * 2**20),
        cost_estimate=pl.CostEstimate(
            flops=2 * lags * count * rows * width * width,
            bytes_accessed=4 * count * rows * width,
            transcendentals=0,
        ),
    )(noise, weights)


def filter_kernel(parts, coded_ref, lat_ref, out_ref, padded, spread):
    shares, _, _ = coded_ref.shape
    rows, width = out_ref.shape
    halves = width // TILE
    held = rows // shares
    strip = held // parts
    taps = spread.shape[0]

    @pl.when(pl.program_id(0) == 0)
    def _():
        empty = jnp.zeros((8 - taps, TILE), jnp.float32)
        for start in range(0, rows, TILE):
            lines = slice(start, start + TILE)
            columns = jnp.concatenate([lat_ref[:, lines], empty], axis=0).T
            for tap in range(taps):
                spread[tap, lines, :] = jnp.broadcast_to(columns[:, tap : tap + 1], (TILE, TILE))

    for share in range(shares):
        side = coded_ref[share, halves * held :].astype(jnp.float32)
        for half in range(halves):
            lanes = slice(half * TILE, (half + 1) * TILE)
            for part in range(parts):
                line = part * halves + half
                scale = jnp.exp2(side[line : line + 1]) * (1.0 / TOP)
                place = 8 + share * held + part * strip
                padded[place : place + strip, lanes] = (
                    coded_ref[share, line * strip : (line + 1) * strip].astype(jnp.float32) * scale
                )
            if share in (0, shares - 1):
                line = SIDE - 3 * halves
                scale = jnp.exp2(side[line + half : line + half + 1]) * (1.0 / TOP)
                line += halves + half * RIM
                place = 8 - RIM if share == 0 else 8 + rows
                padded[place : place + RIM, lanes] = side[line : line + RIM] * scale
    for start in range(0, rows, strip):
        for half in range(halves):
            lanes = slice(half * TILE, (half + 1) * TILE)
            total = None
            for tap in range(taps):
                place = 8 - RIM + tap + start
                term = spread[tap, start : start + strip] * padded[place : place + strip, lanes]
                total = term if total is None else total + term
            out_ref[start : start + strip, lanes] = total


def band_filter(coded, lat_weights, parts, width):
    fields, shares, sent, _ = coded.shape
    taps, rows = lat_weights.shape
    return pl.pallas_call(
        functools.partial(filter_kernel, parts),
        out_shape=jax.ShapeDtypeStruct((fields, rows, width), jnp.float32),
        grid=(fields,),
        in_specs=[
            pl.BlockSpec((None, shares, sent, TILE), lambda f: (f, 0, 0, 0)),
            pl.BlockSpec((taps, rows), lambda f: (0, 0)),
        ],
        out_specs=pl.BlockSpec((None, rows, width), lambda f: (f, 0, 0)),
        scratch_shapes=[
            pltpu.VMEM((rows + 16, width), jnp.float32),
            pltpu.VMEM((taps, rows, TILE), jnp.float32),
        ],
        compiler_params=pltpu.CompilerParams(vmem_limit_bytes=12 * 2**20),
        cost_estimate=pl.CostEstimate(
            flops=10 * fields * rows * width,
            bytes_accessed=6 * fields * rows * width,
            transcendentals=0,
        ),
    )(coded, lat_weights)


def per_device(noise, factors, tile_mask, lat_weights):
    members, levels, rows, width = noise.shape
    fields = members * levels
    bands = factors.shape[1]
    count, lat = lax.axis_size("lon"), lax.axis_size("lat")
    parts = fields * bands // count
    shares = bands // parts
    held = rows // shares
    groups = [[device_at(place) for place in range(count)]]
    joins = []
    for field in range(fields):
        for row in range(lat - 1):
            south = groups[0][field * shares + shares - 1] * lat + row
            north = groups[0][field * shares] * lat + row + 1
            joins += [(south, north), (north, south)]
    mine = lax.all_to_all(
        noise.reshape(count, held, width), "lon", 0, 0, axis_index_groups=groups, tiled=True
    )
    edges, weights = rim(tile_mask.transpose(1, 2, 3, 0), mine, factors, parts, shares)
    other = lax.ppermute(edges, ("lon", "lat"), joins)
    coded = mix(mine, weights)
    own = SIDE - 3 * (width // TILE)
    side = jnp.concatenate([coded[:, -SIDE : own - SIDE], other[:, own:]], axis=1)
    coded = lax.dynamic_update_slice(coded, side, (0, coded.shape[1] - SIDE, 0))
    coded = lax.all_to_all(coded, "lon", 0, 0, axis_index_groups=groups, tiled=True)
    result_field = band_filter(
        coded.reshape(fields, shares, -1, TILE), lat_weights, parts, width
    )
    return result_field.reshape(members, levels, rows, width)


def solution(mesh):
    return jax.shard_map(
        per_device,
        mesh=mesh,
        in_specs=(
            P(None, None, "lat", "lon"),
            P(None, "lat", None, None),
            P(None, "lat", None, None),
            P(None, "lat"),
        ),
        out_specs=P(None, None, "lat", "lon"),
        check_vma=False,
    )
```

```python
import functools

import jax
import jax.numpy as jnp
from jax import lax
from jax.experimental import pallas as pl
from jax.experimental.pallas import tpu as pltpu
from jax.sharding import PartitionSpec as P

TILE = 128
RIM = 2
TOP = 32767.0
SIDE = 16
GROUP = 8


def device_at(place):
    return place // 8 * 8 + place % 4 * 2 + place // 4 % 2


def place_of(device):
    return device // 8 * 8 + device % 2 * 4 + device // 2 % 4


def code(block):
    peak = jnp.maximum(jnp.max(jnp.abs(block), axis=0, keepdims=True), 2.0**-120)
    power = jnp.ceil(jnp.log2(peak) + 1e-5)
    return jnp.round(block * jnp.exp2(-power) * TOP).astype(jnp.int32), power.astype(jnp.int32)


def fill_places(places, count, reach):
    for index in range(count + 2 * reach):
        places[index] = place_of((index + count - reach) % count)


def banded(places, noise_ref, weights, start, group, lines):
    lags = len(weights)
    targets = [device_at(start + g) for g in range(group)]
    total = None
    for lag in range(lags):
        blocks = [noise_ref[places[target + lag], lines, :] for target in targets]
        product = jnp.dot(
            jnp.concatenate(blocks, axis=0), weights[lag][...], preferred_element_type=jnp.float32
        )
        total = product if total is None else total + product
    return total


def rim_kernel(
    shares, mask_ref, noise_ref, factors_ref, side_ref, weights_ref, loaded, sems, places
):
    parts, lags, width, _ = weights_ref.shape
    count, rows, _ = noise_ref.shape
    tiles = width // TILE
    share = place_of(lax.axis_index("lon")) % shares
    last = share == shares - 1
    copies = [
        pltpu.make_async_copy(
            factors_ref.at[:, share * parts + part], loaded.at[part], sems.at[part]
        )
        for part in range(parts)
    ]
    for copy in copies:
        copy.start()
    fill_places(places, count, lags // 2)
    for part in range(parts):
        copies[part].wait()
        for lag in range(lags):
            for a in range(tiles):
                for b in range(tiles):
                    keep = mask_ref[share * parts + part, a, b, lag]
                    keep = keep.astype(jnp.float32).astype(jnp.bfloat16)
                    spot = (pl.ds(a * TILE, TILE), pl.ds(b * TILE, TILE))
                    weights_ref[(part, lag, *spot)] = loaded[(part, lag, *spot)] * keep
    weights = [weights_ref.at[jnp.where(last, parts - 1, 0), lag] for lag in range(lags)]
    line = pl.multiple_of(jnp.where(last, rows - SIDE, 0), SIDE)
    total = banded(places, noise_ref, weights, 0, count, pl.ds(line, SIDE))
    for g in range(count):
        block = total[g * SIDE : (g + 1) * SIDE]
        edge = jnp.where(last, block[SIDE - RIM :], block[:RIM])
        powers, codes = [], []
        for half in range(width // TILE):
            coded, power = code(edge[:, half * TILE : (half + 1) * TILE])
            powers.append(power)
            codes.append(coded)
        empty = jnp.zeros((SIDE - 3 * len(codes), TILE), jnp.int32)
        side_ref[g] = jnp.concatenate([empty] + powers + codes, axis=0).astype(jnp.int16)


def rim(mask, noise, factors, parts, shares):
    count, _, width = noise.shape
    lags = factors.shape[0]
    vmem = pl.BlockSpec(memory_space=pltpu.VMEM)
    held = (parts, lags, width, width)
    return pl.pallas_call(
        functools.partial(rim_kernel, shares),
        out_shape=[
            jax.ShapeDtypeStruct((count, SIDE, TILE), jnp.int16),
            jax.ShapeDtypeStruct(held, factors.dtype),
        ],
        in_specs=[
            pl.BlockSpec(memory_space=pltpu.SMEM),
            vmem,
            pl.BlockSpec(memory_space=pltpu.HBM),
        ],
        out_specs=[vmem] * 2,
        scratch_shapes=[
            pltpu.VMEM(held, factors.dtype),
            pltpu.SemaphoreType.DMA((parts,)),
            pltpu.SMEM((count + lags - 1,), jnp.int32),
        ],
        compiler_params=pltpu.CompilerParams(vmem_limit_bytes=46 * 2**20),
        cost_estimate=pl.CostEstimate(
            flops=2 * lags * count * SIDE * width * width,
            bytes_accessed=4 * count * SIDE * width,
            transcendentals=0,
        ),
    )(mask, noise, factors)


def mix_kernel(noise_ref, weights_ref, lat_ref, coded_ref, spread_ref, powers, places):
    parts, lags, width, _ = weights_ref.shape
    count, rows, _ = noise_ref.shape
    strip = rows // parts
    group = powers.shape[0] // parts
    halves = width // TILE
    part, step = pl.program_id(1), pl.program_id(0)

    @pl.when((part == 0) & (step == 0))
    def _():
        fill_places(places, count, lags // 2)

    weights = [weights_ref.at[part, lag] for lag in range(lags)]
    lines = pl.ds(pl.multiple_of(part * strip, strip), strip)
    total = banded(places, noise_ref, weights, step * group, group, lines)
    taps = spread_ref.shape[0]
    start = pl.multiple_of((step * parts + part) * TILE, TILE)
    empty = jnp.zeros((8 - taps, TILE), jnp.float32)
    columns = jnp.concatenate([lat_ref[:, pl.ds(start, TILE)], empty], axis=0).T
    for tap in range(taps):
        spread_ref[tap, pl.ds(start, TILE), :] = jnp.broadcast_to(
            columns[:, tap : tap + 1], (TILE, TILE)
        )
    for g in range(group):
        block = total[g * strip : (g + 1) * strip]
        for half in range(halves):
            coded, power = code(block[:, half * TILE : (half + 1) * TILE])
            start = pl.multiple_of((part * halves + half) * strip, strip)
            coded_ref[step * group + g, pl.ds(start, strip), :] = coded.astype(jnp.int16)
            powers[part * group + g, half : half + 1, :] = power

    @pl.when(part == parts - 1)
    def _():
        for g in range(group):
            side = [powers[p * group + g, :halves] for p in range(parts)]
            side.append(jnp.zeros((SIDE - parts * halves, TILE), jnp.int32))
            coded_ref[step * group + g, parts * halves * strip :, :] = jnp.concatenate(side, axis=0).astype(
                jnp.int16
            )


def mix(noise, weights, lat_weights):
    count, rows, width = noise.shape
    parts, lags = weights.shape[:2]
    strip = rows // parts
    sent = rows * width // TILE + SIDE
    return pl.pallas_call(
        mix_kernel,
        out_shape=[
            jax.ShapeDtypeStruct((count, sent, TILE), jnp.int16),
            jax.ShapeDtypeStruct((*lat_weights.shape, TILE), jnp.float32),
        ],
        grid=(count // GROUP, parts),
        in_specs=[pl.BlockSpec(memory_space=pltpu.VMEM)] * 3,
        out_specs=[pl.BlockSpec(memory_space=pltpu.VMEM)] * 2,
        scratch_shapes=[
            pltpu.VMEM((parts * GROUP, 8, TILE), jnp.int32),
            pltpu.SMEM((count + lags - 1,), jnp.int32),
        ],
        compiler_params=pltpu.CompilerParams(vmem_limit_bytes=16 * 2**20),
        cost_estimate=pl.CostEstimate(
            flops=2 * lags * count * rows * width * width,
            bytes_accessed=4 * count * rows * width,
            transcendentals=0,
        ),
    )(noise, weights, lat_weights)


def filter_kernel(parts, coded_ref, spread_ref, out_ref, padded):
    shares, _, _ = coded_ref.shape
    rows, width = out_ref.shape
    halves = width // TILE
    held = rows // shares
    strip = held // parts
    taps = spread_ref.shape[0]
    for share in range(shares):
        side = coded_ref[share, halves * held :].astype(jnp.float32)
        for half in range(halves):
            lanes = slice(half * TILE, (half + 1) * TILE)
            for part in range(parts):
                line = part * halves + half
                scale = jnp.exp2(side[line : line + 1]) * (1.0 / TOP)
                place = 8 + share * held + part * strip
                padded[place : place + strip, lanes] = (
                    coded_ref[share, line * strip : (line + 1) * strip].astype(jnp.float32) * scale
                )
            if share in (0, shares - 1):
                line = SIDE - 3 * halves
                scale = jnp.exp2(side[line + half : line + half + 1]) * (1.0 / TOP)
                line += halves + half * RIM
                place = 8 - RIM if share == 0 else 8 + rows
                padded[place : place + RIM, lanes] = side[line : line + RIM] * scale
    for start in range(0, rows, strip):
        for half in range(halves):
            lanes = slice(half * TILE, (half + 1) * TILE)
            total = None
            for tap in range(taps):
                place = 8 - RIM + tap + start
                term = spread_ref[tap, start : start + strip] * padded[place : place + strip, lanes]
                total = term if total is None else total + term
            out_ref[start : start + strip, lanes] = total


def band_filter(coded, spread, parts, width):
    fields, shares, sent, _ = coded.shape
    rows = spread.shape[1]
    return pl.pallas_call(
        functools.partial(filter_kernel, parts),
        out_shape=jax.ShapeDtypeStruct((fields, rows, width), jnp.float32),
        grid=(fields,),
        in_specs=[
            pl.BlockSpec((None, shares, sent, TILE), lambda f: (f, 0, 0, 0)),
            pl.BlockSpec(memory_space=pltpu.VMEM),
        ],
        out_specs=pl.BlockSpec((None, rows, width), lambda f: (f, 0, 0)),
        scratch_shapes=[
            pltpu.VMEM((rows + 16, width), jnp.float32),
        ],
        compiler_params=pltpu.CompilerParams(vmem_limit_bytes=10 * 2**20),
        cost_estimate=pl.CostEstimate(
            flops=10 * fields * rows * width,
            bytes_accessed=6 * fields * rows * width,
            transcendentals=0,
        ),
    )(coded, spread)


def per_device(noise, factors, tile_mask, lat_weights):
    members, levels, rows, width = noise.shape
    fields = members * levels
    bands = factors.shape[1]
    count, lat = lax.axis_size("lon"), lax.axis_size("lat")
    parts = fields * bands // count
    shares = bands // parts
    held = rows // shares
    groups = [[device_at(place) for place in range(count)]]
    joins = []
    for field in range(fields):
        for row in range(lat - 1):
            south = groups[0][field * shares + shares - 1] * lat + row
            north = groups[0][field * shares] * lat + row + 1
            joins += [(south, north), (north, south)]
    mine = lax.all_to_all(
        noise.reshape(count, held, width), "lon", 0, 0, axis_index_groups=groups, tiled=True
    )
    edges, weights = rim(tile_mask.transpose(1, 2, 3, 0), mine, factors, parts, shares)
    other = lax.ppermute(edges, ("lon", "lat"), joins)
    coded, spread = mix(mine, weights, lat_weights)
    own = SIDE - 3 * (width // TILE)
    side = jnp.concatenate([coded[:, -SIDE : own - SIDE], other[:, own:]], axis=1)
    coded = lax.dynamic_update_slice(coded, side, (0, coded.shape[1] - SIDE, 0))
    coded = lax.all_to_all(coded, "lon", 0, 0, axis_index_groups=groups, tiled=True)
    result_field = band_filter(
        coded.reshape(fields, shares, -1, TILE), spread, parts, width
    )
    return result_field.reshape(members, levels, rows, width)


def solution(mesh):
    return jax.shard_map(
        per_device,
        mesh=mesh,
        in_specs=(
            P(None, None, "lat", "lon"),
            P(None, "lat", None, None),
            P(None, "lat", None, None),
            P(None, "lat"),
        ),
        out_specs=P(None, None, "lat", "lon"),
        check_vma=False,
    )
```

```python
import functools

import jax
import jax.numpy as jnp
from jax import lax
from jax.experimental import pallas as pl
from jax.experimental.pallas import tpu as pltpu
from jax.sharding import PartitionSpec as P

TILE = 128
RIM = 2
TOP = 32767.0
SIDE = 16
GROUP = 16


def device_at(place):
    return place // 8 * 8 + place % 4 * 2 + place // 4 % 2


def place_of(device):
    return device // 8 * 8 + device % 2 * 4 + device // 2 % 4


def code(block):
    peak = jnp.maximum(jnp.max(jnp.abs(block), axis=0, keepdims=True), 2.0**-110)
    power = jnp.ceil(jnp.log2(peak) + 1e-5)
    return jnp.round(block * (jnp.exp2(-power) * TOP)).astype(jnp.int32), power.astype(jnp.int32)


def fill_places(places, count, reach):
    for index in range(count + 2 * reach):
        places[index] = place_of((index + count - reach) % count)


def banded(places, noise_ref, weights, start, group, lines):
    lags = len(weights)
    targets = [device_at(start + g) for g in range(group)]
    total = None
    for lag in range(lags):
        blocks = [noise_ref[places[target + lag], lines, :] for target in targets]
        product = jnp.dot(
            jnp.concatenate(blocks, axis=0), weights[lag][...], preferred_element_type=jnp.float32
        )
        total = product if total is None else total + product
    return total


def rim_kernel(
    shares, mask_ref, noise_ref, factors_ref, side_ref, weights_ref, loaded, sems, places
):
    parts, lags, width, _ = weights_ref.shape
    count, rows, _ = noise_ref.shape
    tiles = width // TILE
    share = place_of(lax.axis_index("lon")) % shares
    last = share == shares - 1
    order = [jnp.where(last, parts - 1 - part, part) for part in range(parts)]
    copies = [
        pltpu.make_async_copy(
            factors_ref.at[:, share * parts + order[index]], loaded.at[index], sems.at[index]
        )
        for index in range(parts)
    ]
    for copy in copies:
        copy.start()
    fill_places(places, count, lags // 2)

    def mask_part(index, part):
        copies[index].wait()
        for lag in range(lags):
            for a in range(tiles):
                for b in range(tiles):
                    keep = mask_ref[share * parts + part, a, b, lag]
                    keep = keep.astype(jnp.float32).astype(jnp.bfloat16)
                    spot = (pl.ds(a * TILE, TILE), pl.ds(b * TILE, TILE))
                    weights_ref[(part, lag, *spot)] = loaded[(index, lag, *spot)] * keep

    mask_part(0, order[0])
    weights = [weights_ref.at[order[0], lag] for lag in range(lags)]
    line = pl.multiple_of(jnp.where(last, rows - SIDE, 0), SIDE)
    total = banded(places, noise_ref, weights, 0, count, pl.ds(line, SIDE))
    for g in range(count):
        block = total[g * SIDE : (g + 1) * SIDE]
        edge = jnp.where(last, block[SIDE - RIM :], block[:RIM])
        powers, codes = [], []
        for half in range(width // TILE):
            coded, power = code(edge[:, half * TILE : (half + 1) * TILE])
            powers.append(power)
            codes.append(coded)
        empty = jnp.zeros((SIDE - 3 * len(codes), TILE), jnp.int32)
        side_ref[g] = jnp.concatenate([empty] + powers + codes, axis=0).astype(jnp.int16)
    for index in range(1, parts):
        mask_part(index, order[index])


def rim(mask, noise, factors, parts, shares):
    count, _, width = noise.shape
    lags = factors.shape[0]
    vmem = pl.BlockSpec(memory_space=pltpu.VMEM)
    held = (parts, lags, width, width)
    return pl.pallas_call(
        functools.partial(rim_kernel, shares),
        out_shape=[
            jax.ShapeDtypeStruct((count, SIDE, TILE), jnp.int16),
            jax.ShapeDtypeStruct(held, factors.dtype),
        ],
        in_specs=[
            pl.BlockSpec(memory_space=pltpu.SMEM),
            vmem,
            pl.BlockSpec(memory_space=pltpu.HBM),
        ],
        out_specs=[vmem] * 2,
        scratch_shapes=[
            pltpu.VMEM(held, factors.dtype),
            pltpu.SemaphoreType.DMA((parts,)),
            pltpu.SMEM((count + lags - 1,), jnp.int32),
        ],
        compiler_params=pltpu.CompilerParams(vmem_limit_bytes=46 * 2**20),
        cost_estimate=pl.CostEstimate(
            flops=2 * lags * count * SIDE * width * width,
            bytes_accessed=4 * count * SIDE * width,
            transcendentals=0,
        ),
    )(mask, noise, factors)


def mix_kernel(noise_ref, weights_ref, lat_ref, coded_ref, spread_ref, powers, places):
    parts, lags, width, _ = weights_ref.shape
    count, rows, _ = noise_ref.shape
    strip = rows // parts
    group = powers.shape[0] // parts
    halves = width // TILE
    part, step = pl.program_id(1), pl.program_id(0)

    @pl.when((part == 0) & (step == 0))
    def _():
        fill_places(places, count, lags // 2)

    weights = [weights_ref.at[part, lag] for lag in range(lags)]
    lines = pl.ds(pl.multiple_of(part * strip, strip), strip)
    total = banded(places, noise_ref, weights, step * group, group, lines)
    taps = spread_ref.shape[0]
    empty = jnp.zeros((8 - taps, TILE), jnp.float32)
    pieces = spread_ref.shape[1] // TILE * group // (count * parts)
    for piece in range(pieces):
        start = pl.multiple_of(((step * parts + part) * pieces + piece) * TILE, TILE)
        columns = jnp.concatenate([lat_ref[:, pl.ds(start, TILE)], empty], axis=0).T
        for tap in range(taps):
            spread_ref[tap, pl.ds(start, TILE), :] = jnp.broadcast_to(
                columns[:, tap : tap + 1], (TILE, TILE)
            )
    for g in range(group):
        block = total[g * strip : (g + 1) * strip]
        for half in range(halves):
            coded, power = code(block[:, half * TILE : (half + 1) * TILE])
            start = pl.multiple_of((part * halves + half) * strip, strip)
            coded_ref[step * group + g, pl.ds(start, strip), :] = coded.astype(jnp.int16)
            powers[part * group + g, half : half + 1, :] = power

    @pl.when(part == parts - 1)
    def _():
        for g in range(group):
            side = [powers[p * group + g, :halves] for p in range(parts)]
            side.append(jnp.zeros((SIDE - parts * halves, TILE), jnp.int32))
            coded_ref[step * group + g, parts * halves * strip :, :] = jnp.concatenate(side, axis=0).astype(
                jnp.int16
            )


def mix(noise, weights, lat_weights):
    count, rows, width = noise.shape
    parts, lags = weights.shape[:2]
    strip = rows // parts
    sent = rows * width // TILE + SIDE
    return pl.pallas_call(
        mix_kernel,
        out_shape=[
            jax.ShapeDtypeStruct((count, sent, TILE), jnp.int16),
            jax.ShapeDtypeStruct((*lat_weights.shape, TILE), jnp.float32),
        ],
        grid=(count // GROUP, parts),
        in_specs=[pl.BlockSpec(memory_space=pltpu.VMEM)] * 3,
        out_specs=[pl.BlockSpec(memory_space=pltpu.VMEM)] * 2,
        scratch_shapes=[
            pltpu.VMEM((parts * GROUP, 8, TILE), jnp.int32),
            pltpu.SMEM((count + lags - 1,), jnp.int32),
        ],
        compiler_params=pltpu.CompilerParams(vmem_limit_bytes=16 * 2**20),
        cost_estimate=pl.CostEstimate(
            flops=2 * lags * count * rows * width * width,
            bytes_accessed=4 * count * rows * width,
            transcendentals=0,
        ),
    )(noise, weights, lat_weights)


def filter_kernel(parts, coded_ref, spread_ref, out_ref, padded):
    shares, _, _ = coded_ref.shape
    rows, width = out_ref.shape
    halves = width // TILE
    held = rows // shares
    strip = held // parts
    taps = spread_ref.shape[0]
    for share in range(shares):
        side = coded_ref[share, halves * held :].astype(jnp.float32)
        for half in range(halves):
            lanes = slice(half * TILE, (half + 1) * TILE)
            for part in range(parts):
                line = part * halves + half
                scale = jnp.exp2(side[line : line + 1]) * (1.0 / TOP)
                place = 8 + share * held + part * strip
                padded[place : place + strip, lanes] = (
                    coded_ref[share, line * strip : (line + 1) * strip].astype(jnp.float32) * scale
                )
            if share in (0, shares - 1):
                line = SIDE - 3 * halves
                scale = jnp.exp2(side[line + half : line + half + 1]) * (1.0 / TOP)
                line += halves + half * RIM
                place = 8 - RIM if share == 0 else 8 + rows
                padded[place : place + RIM, lanes] = side[line : line + RIM] * scale
    for start in range(0, rows, strip):
        for half in range(halves):
            lanes = slice(half * TILE, (half + 1) * TILE)
            total = None
            for tap in range(taps):
                place = 8 - RIM + tap + start
                term = spread_ref[tap, start : start + strip] * padded[place : place + strip, lanes]
                total = term if total is None else total + term
            out_ref[start : start + strip, lanes] = total


def band_filter(coded, spread, parts, width):
    fields, shares, sent, _ = coded.shape
    rows = spread.shape[1]
    return pl.pallas_call(
        functools.partial(filter_kernel, parts),
        out_shape=jax.ShapeDtypeStruct((fields, rows, width), jnp.float32),
        grid=(fields,),
        in_specs=[
            pl.BlockSpec((None, shares, sent, TILE), lambda f: (f, 0, 0, 0)),
            pl.BlockSpec(memory_space=pltpu.VMEM),
        ],
        out_specs=pl.BlockSpec((None, rows, width), lambda f: (f, 0, 0)),
        scratch_shapes=[
            pltpu.VMEM((rows + 16, width), jnp.float32),
        ],
        compiler_params=pltpu.CompilerParams(vmem_limit_bytes=10 * 2**20),
        cost_estimate=pl.CostEstimate(
            flops=10 * fields * rows * width,
            bytes_accessed=6 * fields * rows * width,
            transcendentals=0,
        ),
    )(coded, spread)


def per_device(noise, factors, tile_mask, lat_weights):
    members, levels, rows, width = noise.shape
    fields = members * levels
    bands = factors.shape[1]
    count, lat = lax.axis_size("lon"), lax.axis_size("lat")
    parts = fields * bands // count
    shares = bands // parts
    held = rows // shares
    groups = [[device_at(place) for place in range(count)]]
    joins = []
    for field in range(fields):
        for row in range(lat - 1):
            south = groups[0][field * shares + shares - 1] * lat + row
            north = groups[0][field * shares] * lat + row + 1
            joins += [(south, north), (north, south)]
    mine = lax.all_to_all(
        noise.reshape(count, held, width), "lon", 0, 0, axis_index_groups=groups, tiled=True
    )
    edges, weights = rim(tile_mask.transpose(1, 2, 3, 0), mine, factors, parts, shares)
    other = lax.ppermute(edges, ("lon", "lat"), joins)
    coded, spread = mix(mine, weights, lat_weights)
    own = SIDE - 3 * (width // TILE)
    side = jnp.concatenate([coded[:, -SIDE : own - SIDE], other[:, own:]], axis=1)
    coded = lax.dynamic_update_slice(coded, side, (0, coded.shape[1] - SIDE, 0))
    coded = lax.all_to_all(coded, "lon", 0, 0, axis_index_groups=groups, tiled=True)
    result_field = band_filter(
        coded.reshape(fields, shares, -1, TILE), spread, parts, width
    )
    return result_field.reshape(members, levels, rows, width)


def solution(mesh):
    return jax.shard_map(
        per_device,
        mesh=mesh,
        in_specs=(
            P(None, None, "lat", "lon"),
            P(None, "lat", None, None),
            P(None, "lat", None, None),
            P(None, "lat"),
        ),
        out_specs=P(None, None, "lat", "lon"),
        check_vma=False,
    )
```

```python
import functools

import jax
import jax.numpy as jnp
from jax import lax
from jax.experimental import pallas as pl
from jax.experimental.pallas import tpu as pltpu
from jax.sharding import PartitionSpec as P

TILE = 128
RIM = 2
TOP = 32767.0
SIDE = 16
GROUP = 16


def device_at(place):
    return place % 4 * 8 + place // 8 * 2 + place // 4 % 2


def place_of(device):
    return device // 2 % 4 * 8 + device % 2 * 4 + device // 8


def code(block):
    peak = jnp.maximum(jnp.max(jnp.abs(block), axis=0, keepdims=True), 2.0**-110)
    power = jnp.ceil(jnp.log2(peak) + 1e-5)
    return jnp.round(block * (jnp.exp2(-power) * TOP)).astype(jnp.int32), power.astype(jnp.int32)


def fill_places(places, count, reach):
    for index in range(count + 2 * reach):
        places[index] = place_of((index + count - reach) % count)


def banded(places, noise_ref, weights, start, group, lines):
    lags = len(weights)
    targets = [device_at(start + g) for g in range(group)]
    total = None
    for lag in range(lags):
        blocks = [noise_ref[places[target + lag], lines, :] for target in targets]
        product = jnp.dot(
            jnp.concatenate(blocks, axis=0), weights[lag][...], preferred_element_type=jnp.float32
        )
        total = product if total is None else total + product
    return total


def rim_kernel(
    shares, mask_ref, noise_ref, factors_ref, side_ref, weights_ref, loaded, sems, places
):
    parts, lags, width, _ = weights_ref.shape
    count, rows, _ = noise_ref.shape
    tiles = width // TILE
    share = place_of(lax.axis_index("lon")) % shares
    last = share == shares - 1
    order = [jnp.where(last, parts - 1 - part, part) for part in range(parts)]
    copies = [
        pltpu.make_async_copy(
            factors_ref.at[:, share * parts + order[index]], loaded.at[index], sems.at[index]
        )
        for index in range(parts)
    ]
    for copy in copies:
        copy.start()
    fill_places(places, count, lags // 2)

    def mask_part(index, part):
        copies[index].wait()
        for lag in range(lags):
            for a in range(tiles):
                for b in range(tiles):
                    keep = mask_ref[share * parts + part, a, b, lag]
                    keep = keep.astype(jnp.float32).astype(jnp.bfloat16)
                    spot = (pl.ds(a * TILE, TILE), pl.ds(b * TILE, TILE))
                    weights_ref[(part, lag, *spot)] = loaded[(index, lag, *spot)] * keep

    mask_part(0, order[0])
    weights = [weights_ref.at[order[0], lag] for lag in range(lags)]
    line = pl.multiple_of(jnp.where(last, rows - SIDE, 0), SIDE)
    total = banded(places, noise_ref, weights, 0, count, pl.ds(line, SIDE))
    for g in range(count):
        block = total[g * SIDE : (g + 1) * SIDE]
        edge = jnp.where(last, block[SIDE - RIM :], block[:RIM])
        powers, codes = [], []
        for half in range(width // TILE):
            coded, power = code(edge[:, half * TILE : (half + 1) * TILE])
            powers.append(power)
            codes.append(coded)
        empty = jnp.zeros((SIDE - 3 * len(codes), TILE), jnp.int32)
        side_ref[g] = jnp.concatenate([empty] + powers + codes, axis=0).astype(jnp.int16)
    for index in range(1, parts):
        mask_part(index, order[index])


def rim(mask, noise, factors, parts, shares):
    count, _, width = noise.shape
    lags = factors.shape[0]
    vmem = pl.BlockSpec(memory_space=pltpu.VMEM)
    held = (parts, lags, width, width)
    return pl.pallas_call(
        functools.partial(rim_kernel, shares),
        out_shape=[
            jax.ShapeDtypeStruct((count, SIDE, TILE), jnp.int16),
            jax.ShapeDtypeStruct(held, factors.dtype),
        ],
        in_specs=[
            pl.BlockSpec(memory_space=pltpu.SMEM),
            vmem,
            pl.BlockSpec(memory_space=pltpu.HBM),
        ],
        out_specs=[vmem] * 2,
        scratch_shapes=[
            pltpu.VMEM(held, factors.dtype),
            pltpu.SemaphoreType.DMA((parts,)),
            pltpu.SMEM((count + lags - 1,), jnp.int32),
        ],
        compiler_params=pltpu.CompilerParams(vmem_limit_bytes=46 * 2**20),
        cost_estimate=pl.CostEstimate(
            flops=2 * lags * count * SIDE * width * width,
            bytes_accessed=4 * count * SIDE * width,
            transcendentals=0,
        ),
    )(mask, noise, factors)


def mix_kernel(noise_ref, weights_ref, lat_ref, coded_ref, spread_ref, powers, places):
    parts, lags, width, _ = weights_ref.shape
    count, rows, _ = noise_ref.shape
    strip = rows // parts
    group = powers.shape[0] // parts
    halves = width // TILE
    part, step = pl.program_id(1), pl.program_id(0)

    @pl.when((part == 0) & (step == 0))
    def _():
        fill_places(places, count, lags // 2)

    weights = [weights_ref.at[part, lag] for lag in range(lags)]
    lines = pl.ds(pl.multiple_of(part * strip, strip), strip)
    total = banded(places, noise_ref, weights, step * group, group, lines)
    taps = spread_ref.shape[0]
    empty = jnp.zeros((8 - taps, TILE), jnp.float32)
    pieces = spread_ref.shape[1] // TILE * group // (count * parts)
    for piece in range(pieces):
        start = pl.multiple_of(((step * parts + part) * pieces + piece) * TILE, TILE)
        columns = jnp.concatenate([lat_ref[:, pl.ds(start, TILE)], empty], axis=0).T
        for tap in range(taps):
            spread_ref[tap, pl.ds(start, TILE), :] = jnp.broadcast_to(
                columns[:, tap : tap + 1], (TILE, TILE)
            )
    for g in range(group):
        block = total[g * strip : (g + 1) * strip]
        for half in range(halves):
            coded, power = code(block[:, half * TILE : (half + 1) * TILE])
            start = pl.multiple_of((part * halves + half) * strip, strip)
            coded_ref[step * group + g, pl.ds(start, strip), :] = coded.astype(jnp.int16)
            powers[part * group + g, half : half + 1, :] = power

    @pl.when(part == parts - 1)
    def _():
        for g in range(group):
            side = [powers[p * group + g, :halves] for p in range(parts)]
            side.append(jnp.zeros((SIDE - parts * halves, TILE), jnp.int32))
            coded_ref[step * group + g, parts * halves * strip :, :] = jnp.concatenate(side, axis=0).astype(
                jnp.int16
            )


def mix(noise, weights, lat_weights):
    count, rows, width = noise.shape
    parts, lags = weights.shape[:2]
    strip = rows // parts
    sent = rows * width // TILE + SIDE
    return pl.pallas_call(
        mix_kernel,
        out_shape=[
            jax.ShapeDtypeStruct((count, sent, TILE), jnp.int16),
            jax.ShapeDtypeStruct((*lat_weights.shape, TILE), jnp.float32),
        ],
        grid=(count // GROUP, parts),
        in_specs=[pl.BlockSpec(memory_space=pltpu.VMEM)] * 3,
        out_specs=[pl.BlockSpec(memory_space=pltpu.VMEM)] * 2,
        scratch_shapes=[
            pltpu.VMEM((parts * GROUP, 8, TILE), jnp.int32),
            pltpu.SMEM((count + lags - 1,), jnp.int32),
        ],
        compiler_params=pltpu.CompilerParams(vmem_limit_bytes=16 * 2**20),
        cost_estimate=pl.CostEstimate(
            flops=2 * lags * count * rows * width * width,
            bytes_accessed=4 * count * rows * width,
            transcendentals=0,
        ),
    )(noise, weights, lat_weights)


def filter_kernel(parts, coded_ref, spread_ref, out_ref, padded):
    shares, _, _ = coded_ref.shape
    rows, width = out_ref.shape
    halves = width // TILE
    held = rows // shares
    strip = held // parts
    taps = spread_ref.shape[0]
    for share in range(shares):
        side = coded_ref[share, halves * held :].astype(jnp.float32)
        for half in range(halves):
            lanes = slice(half * TILE, (half + 1) * TILE)
            for part in range(parts):
                line = part * halves + half
                scale = jnp.exp2(side[line : line + 1]) * (1.0 / TOP)
                place = 8 + share * held + part * strip
                padded[place : place + strip, lanes] = (
                    coded_ref[share, line * strip : (line + 1) * strip].astype(jnp.float32) * scale
                )
            if share in (0, shares - 1):
                line = SIDE - 3 * halves
                scale = jnp.exp2(side[line + half : line + half + 1]) * (1.0 / TOP)
                line += halves + half * RIM
                place = 8 - RIM if share == 0 else 8 + rows
                padded[place : place + RIM, lanes] = side[line : line + RIM] * scale
    for start in range(0, rows, strip):
        for half in range(halves):
            lanes = slice(half * TILE, (half + 1) * TILE)
            total = None
            for tap in range(taps):
                place = 8 - RIM + tap + start
                term = spread_ref[tap, start : start + strip] * padded[place : place + strip, lanes]
                total = term if total is None else total + term
            out_ref[start : start + strip, lanes] = total


def band_filter(coded, spread, parts, width):
    fields, shares, sent, _ = coded.shape
    rows = spread.shape[1]
    return pl.pallas_call(
        functools.partial(filter_kernel, parts),
        out_shape=jax.ShapeDtypeStruct((fields, rows, width), jnp.float32),
        grid=(fields,),
        in_specs=[
            pl.BlockSpec((None, shares, sent, TILE), lambda f: (f, 0, 0, 0)),
            pl.BlockSpec(memory_space=pltpu.VMEM),
        ],
        out_specs=pl.BlockSpec((None, rows, width), lambda f: (f, 0, 0)),
        scratch_shapes=[
            pltpu.VMEM((rows + 16, width), jnp.float32),
        ],
        compiler_params=pltpu.CompilerParams(vmem_limit_bytes=10 * 2**20),
        cost_estimate=pl.CostEstimate(
            flops=10 * fields * rows * width,
            bytes_accessed=6 * fields * rows * width,
            transcendentals=0,
        ),
    )(coded, spread)


def per_device(noise, factors, tile_mask, lat_weights):
    members, levels, rows, width = noise.shape
    fields = members * levels
    bands = factors.shape[1]
    count, lat = lax.axis_size("lon"), lax.axis_size("lat")
    parts = fields * bands // count
    shares = bands // parts
    held = rows // shares
    groups = [[device_at(place) for place in range(count)]]
    joins = []
    for field in range(fields):
        for row in range(lat - 1):
            south = groups[0][field * shares + shares - 1] * lat + row
            north = groups[0][field * shares] * lat + row + 1
            joins += [(south, north), (north, south)]
    mine = lax.all_to_all(
        noise.reshape(count, held, width), "lon", 0, 0, axis_index_groups=groups, tiled=True
    )
    edges, weights = rim(tile_mask.transpose(1, 2, 3, 0), mine, factors, parts, shares)
    other = lax.ppermute(edges, ("lon", "lat"), joins)
    coded, spread = mix(mine, weights, lat_weights)
    own = SIDE - 3 * (width // TILE)
    side = jnp.concatenate([coded[:, -SIDE : own - SIDE], other[:, own:]], axis=1)
    coded = lax.dynamic_update_slice(coded, side, (0, coded.shape[1] - SIDE, 0))
    coded = lax.all_to_all(coded, "lon", 0, 0, axis_index_groups=groups, tiled=True)
    result_field = band_filter(
        coded.reshape(fields, shares, -1, TILE), spread, parts, width
    )
    return result_field.reshape(members, levels, rows, width)


def solution(mesh):
    return jax.shard_map(
        per_device,
        mesh=mesh,
        in_specs=(
            P(None, None, "lat", "lon"),
            P(None, "lat", None, None),
            P(None, "lat", None, None),
            P(None, "lat"),
        ),
        out_specs=P(None, None, "lat", "lon"),
        check_vma=False,
    )
```

```python
import functools

import jax
import jax.numpy as jnp
from jax import lax
from jax.experimental import pallas as pl
from jax.experimental.pallas import tpu as pltpu
from jax.sharding import PartitionSpec as P

TILE = 128
RIM = 2
TOP = 32767.0
SIDE = 16
GROUP = 32


def device_at(place):
    return place % 4 * 8 + place // 8 * 2 + place // 4 % 2


def place_of(device):
    return device // 2 % 4 * 8 + device % 2 * 4 + device // 8


def code(block):
    peak = jnp.maximum(jnp.max(jnp.abs(block), axis=0, keepdims=True), 2.0**-110)
    power = jnp.ceil(jnp.log2(peak) + 1e-5)
    return jnp.round(block * (jnp.exp2(-power) * TOP)).astype(jnp.int32), power.astype(jnp.int32)


def fill_places(places, count, reach):
    for index in range(count + 2 * reach):
        places[index] = place_of((index + count - reach) % count)


def banded(places, noise_ref, weights, start, group, lines):
    lags = len(weights)
    targets = [device_at(start + g) for g in range(group)]
    total = None
    for lag in range(lags):
        blocks = [noise_ref[places[target + lag], lines, :] for target in targets]
        product = jnp.dot(
            jnp.concatenate(blocks, axis=0), weights[lag][...], preferred_element_type=jnp.float32
        )
        total = product if total is None else total + product
    return total


def rim_kernel(
    shares, mask_ref, noise_ref, factors_ref, side_ref, weights_ref, loaded, sems, places
):
    parts, lags, width, _ = weights_ref.shape
    count, rows, _ = noise_ref.shape
    tiles = width // TILE
    share = place_of(lax.axis_index("lon")) % shares
    last = share == shares - 1
    order = [jnp.where(last, parts - 1 - part, part) for part in range(parts)]
    copies = [
        pltpu.make_async_copy(
            factors_ref.at[:, share * parts + order[index]], loaded.at[index], sems.at[index]
        )
        for index in range(parts)
    ]
    for copy in copies:
        copy.start()
    fill_places(places, count, lags // 2)

    def mask_part(index, part):
        copies[index].wait()
        for lag in range(lags):
            for a in range(tiles):
                for b in range(tiles):
                    keep = mask_ref[share * parts + part, a, b, lag]
                    keep = keep.astype(jnp.float32).astype(jnp.bfloat16)
                    spot = (pl.ds(a * TILE, TILE), pl.ds(b * TILE, TILE))
                    weights_ref[(part, lag, *spot)] = loaded[(index, lag, *spot)] * keep

    mask_part(0, order[0])
    weights = [weights_ref.at[order[0], lag] for lag in range(lags)]
    line = pl.multiple_of(jnp.where(last, rows - SIDE, 0), SIDE)
    total = banded(places, noise_ref, weights, 0, count, pl.ds(line, SIDE))
    for g in range(count):
        block = total[g * SIDE : (g + 1) * SIDE]
        edge = jnp.where(last, block[SIDE - RIM :], block[:RIM])
        powers, codes = [], []
        for half in range(width // TILE):
            coded, power = code(edge[:, half * TILE : (half + 1) * TILE])
            powers.append(power)
            codes.append(coded)
        empty = jnp.zeros((SIDE - 3 * len(codes), TILE), jnp.int32)
        side_ref[g] = jnp.concatenate([empty] + powers + codes, axis=0).astype(jnp.int16)
    for index in range(1, parts):
        mask_part(index, order[index])


def rim(mask, noise, factors, parts, shares):
    count, _, width = noise.shape
    lags = factors.shape[0]
    vmem = pl.BlockSpec(memory_space=pltpu.VMEM)
    held = (parts, lags, width, width)
    return pl.pallas_call(
        functools.partial(rim_kernel, shares),
        out_shape=[
            jax.ShapeDtypeStruct((count, SIDE, TILE), jnp.int16),
            jax.ShapeDtypeStruct(held, factors.dtype),
        ],
        in_specs=[
            pl.BlockSpec(memory_space=pltpu.SMEM),
            vmem,
            pl.BlockSpec(memory_space=pltpu.HBM),
        ],
        out_specs=[vmem] * 2,
        scratch_shapes=[
            pltpu.VMEM(held, factors.dtype),
            pltpu.SemaphoreType.DMA((parts,)),
            pltpu.SMEM((count + lags - 1,), jnp.int32),
        ],
        compiler_params=pltpu.CompilerParams(vmem_limit_bytes=46 * 2**20),
        cost_estimate=pl.CostEstimate(
            flops=2 * lags * count * SIDE * width * width,
            bytes_accessed=4 * count * SIDE * width,
            transcendentals=0,
        ),
    )(mask, noise, factors)


def mix_kernel(noise_ref, weights_ref, lat_ref, coded_ref, spread_ref, powers, places):
    parts, lags, width, _ = weights_ref.shape
    count, rows, _ = noise_ref.shape
    strip = rows // parts
    group = powers.shape[0] // parts
    halves = width // TILE
    part, step = pl.program_id(1), pl.program_id(0)

    @pl.when((part == 0) & (step == 0))
    def _():
        fill_places(places, count, lags // 2)

    weights = [weights_ref.at[part, lag] for lag in range(lags)]
    lines = pl.ds(pl.multiple_of(part * strip, strip), strip)
    total = banded(places, noise_ref, weights, step * group, group, lines)
    taps = spread_ref.shape[0]
    empty = jnp.zeros((8 - taps, TILE), jnp.float32)
    pieces = spread_ref.shape[1] // TILE * group // (count * parts)
    for piece in range(pieces):
        start = pl.multiple_of(((step * parts + part) * pieces + piece) * TILE, TILE)
        columns = jnp.concatenate([lat_ref[:, pl.ds(start, TILE)], empty], axis=0).T
        for tap in range(taps):
            spread_ref[tap, pl.ds(start, TILE), :] = jnp.broadcast_to(
                columns[:, tap : tap + 1], (TILE, TILE)
            )
    for g in range(group):
        block = total[g * strip : (g + 1) * strip]
        for half in range(halves):
            coded, power = code(block[:, half * TILE : (half + 1) * TILE])
            start = pl.multiple_of((part * halves + half) * strip, strip)
            coded_ref[step * group + g, pl.ds(start, strip), :] = coded.astype(jnp.int16)
            powers[part * group + g, half : half + 1, :] = power

    @pl.when(part == parts - 1)
    def _():
        for g in range(group):
            side = [powers[p * group + g, :halves] for p in range(parts)]
            side.append(jnp.zeros((SIDE - parts * halves, TILE), jnp.int32))
            coded_ref[step * group + g, parts * halves * strip :, :] = jnp.concatenate(side, axis=0).astype(
                jnp.int16
            )


def mix(noise, weights, lat_weights):
    count, rows, width = noise.shape
    parts, lags = weights.shape[:2]
    strip = rows // parts
    sent = rows * width // TILE + SIDE
    return pl.pallas_call(
        mix_kernel,
        out_shape=[
            jax.ShapeDtypeStruct((count, sent, TILE), jnp.int16),
            jax.ShapeDtypeStruct((*lat_weights.shape, TILE), jnp.float32),
        ],
        grid=(count // GROUP, parts),
        in_specs=[pl.BlockSpec(memory_space=pltpu.VMEM)] * 3,
        out_specs=[pl.BlockSpec(memory_space=pltpu.VMEM)] * 2,
        scratch_shapes=[
            pltpu.VMEM((parts * GROUP, 8, TILE), jnp.int32),
            pltpu.SMEM((count + lags - 1,), jnp.int32),
        ],
        compiler_params=pltpu.CompilerParams(vmem_limit_bytes=24 * 2**20),
        cost_estimate=pl.CostEstimate(
            flops=2 * lags * count * rows * width * width,
            bytes_accessed=4 * count * rows * width,
            transcendentals=0,
        ),
    )(noise, weights, lat_weights)


def filter_kernel(parts, coded_ref, spread_ref, out_ref, padded):
    shares, _, _ = coded_ref.shape
    rows, width = out_ref.shape
    halves = width // TILE
    held = rows // shares
    strip = held // parts
    taps = spread_ref.shape[0]
    for share in range(shares):
        side = coded_ref[share, halves * held :].astype(jnp.float32)
        for half in range(halves):
            lanes = slice(half * TILE, (half + 1) * TILE)
            for part in range(parts):
                line = part * halves + half
                scale = jnp.exp2(side[line : line + 1]) * (1.0 / TOP)
                place = 8 + share * held + part * strip
                padded[place : place + strip, lanes] = (
                    coded_ref[share, line * strip : (line + 1) * strip].astype(jnp.float32) * scale
                )
            if share in (0, shares - 1):
                line = SIDE - 3 * halves
                scale = jnp.exp2(side[line + half : line + half + 1]) * (1.0 / TOP)
                line += halves + half * RIM
                place = 8 - RIM if share == 0 else 8 + rows
                padded[place : place + RIM, lanes] = side[line : line + RIM] * scale
    for start in range(0, rows, strip):
        for half in range(halves):
            lanes = slice(half * TILE, (half + 1) * TILE)
            total = None
            for tap in range(taps):
                place = 8 - RIM + tap + start
                term = spread_ref[tap, start : start + strip] * padded[place : place + strip, lanes]
                total = term if total is None else total + term
            out_ref[start : start + strip, lanes] = total


def band_filter(coded, spread, parts, width):
    fields, shares, sent, _ = coded.shape
    rows = spread.shape[1]
    return pl.pallas_call(
        functools.partial(filter_kernel, parts),
        out_shape=jax.ShapeDtypeStruct((fields, rows, width), jnp.float32),
        grid=(fields,),
        in_specs=[
            pl.BlockSpec((None, shares, sent, TILE), lambda f: (f, 0, 0, 0)),
            pl.BlockSpec(memory_space=pltpu.VMEM),
        ],
        out_specs=pl.BlockSpec((None, rows, width), lambda f: (f, 0, 0)),
        scratch_shapes=[
            pltpu.VMEM((rows + 16, width), jnp.float32),
        ],
        compiler_params=pltpu.CompilerParams(vmem_limit_bytes=10 * 2**20),
        cost_estimate=pl.CostEstimate(
            flops=10 * fields * rows * width,
            bytes_accessed=6 * fields * rows * width,
            transcendentals=0,
        ),
    )(coded, spread)


def per_device(noise, factors, tile_mask, lat_weights):
    members, levels, rows, width = noise.shape
    fields = members * levels
    bands = factors.shape[1]
    count, lat = lax.axis_size("lon"), lax.axis_size("lat")
    parts = fields * bands // count
    shares = bands // parts
    held = rows // shares
    groups = [[device_at(place) for place in range(count)]]
    joins = []
    for field in range(fields):
        for row in range(lat - 1):
            south = groups[0][field * shares + shares - 1] * lat + row
            north = groups[0][field * shares] * lat + row + 1
            joins += [(south, north), (north, south)]
    mine = lax.all_to_all(
        noise.reshape(count, held, width), "lon", 0, 0, axis_index_groups=groups, tiled=True
    )
    edges, weights = rim(tile_mask.transpose(1, 2, 3, 0), mine, factors, parts, shares)
    other = lax.ppermute(edges, ("lon", "lat"), joins)
    coded, spread = mix(mine, weights, lat_weights)
    own = SIDE - 3 * (width // TILE)
    side = jnp.concatenate([coded[:, -SIDE : own - SIDE], other[:, own:]], axis=1)
    coded = lax.dynamic_update_slice(coded, side, (0, coded.shape[1] - SIDE, 0))
    coded = lax.all_to_all(coded, "lon", 0, 0, axis_index_groups=groups, tiled=True)
    result_field = band_filter(
        coded.reshape(fields, shares, -1, TILE), spread, parts, width
    )
    return result_field.reshape(members, levels, rows, width)


def solution(mesh):
    return jax.shard_map(
        per_device,
        mesh=mesh,
        in_specs=(
            P(None, None, "lat", "lon"),
            P(None, "lat", None, None),
            P(None, "lat", None, None),
            P(None, "lat"),
        ),
        out_specs=P(None, None, "lat", "lon"),
        check_vma=False,
    )
```
